32 devices in a mesh: groups: 2 (over y), samples: 4 (over z), snps: 4 (over x, core).
Axes of the slice: x: 2, y: 2, z: 4, core: 2. Of those that a mesh axis runs over, the one named last changes fastest.
Arguments:
- genotype: int32 [16384, 768], P(('groups', 'samples'), 'snps'), parts along dimension 0, may hold values from 0 to 170, as said below
- traits: bfloat16 [16384, 512], P(('groups', 'samples')), parts along dimension 0, may hold values from -6 to 6
- sample_mask: int32 [16384], P(('groups', 'samples')), parts along dimension 0, may hold values from 0 to 1
- block_ids: int32 [6144], P(('groups', 'snps')), parts along dimension 0, may hold values from 0 to 1, never falling along the last dimension, each value on 1 to 2304 neighbouring positions
- running_total: float32 [1024, 512], P(('groups', 'samples', 'snps')), parts along dimension 0, may hold values from -6 to 6
Outputs:
- assoc: float32 [4, 1536, 512], P('snps', ('groups', 'samples')), parts along dimension 1
- block_gram: float32 [2, 1024, 512], P(None, ('groups', 'samples', 'snps')), parts along dimension 1
- total: float32 [1024, 512], P(('groups', 'samples', 'snps')), parts along dimension 0
The draws below stay inside these ranges and needn't reach their ends.
There are 2 independent parts, one for each index of `groups`. The reference program is written for one: setup_inputs(seed, part) draws one part's arguments, and reference() takes and returns one part's arrays. A program takes and returns all parts, laid end to end along the dimension named above; each array names one. Nothing has to cross between parts.
Inputs may be any that keep to these rules, and one draw needn't show every extreme that they name: `genotype`: each word holds 4 dosages of 0 to 2, SNP 4 w + f in bits 2 f and 2 f + 1 of word w; the pattern 3 never occurs. `block_ids`: never falling; each of the 2 blocks occurs.
All inputs are finite; a program needn't handle non-finite values.
Results may differ from the reference program's by a relative error of at most 0.0019.
Values may be sent and summed in bfloat16 or wider, within the bound.
A program may use at most 64 MiB of HBM per device.

```python
import math
import jax
import jax.numpy as jnp
import numpy as np
from jax import lax

K = 512
SNP_DEV = 768
BLOCKS = 2
SAMPLES = 8192
SNPS = 3072
N_SNPS = 4


def draw_genotype(key, part):
    key = jax.random.fold_in(key, 11)
    key_freq, key_dose = jax.random.split(key)
    width = SNPS // 4
    freq = jax.random.randint(key_freq, (width, 4), 50, 501, dtype=jnp.int32)
    packed = jnp.zeros((SAMPLES, width), jnp.int32)
    for field in range(4):
        key_first, key_second = jax.random.split(jax.random.fold_in(key_dose, field))
        first = (jax.random.randint(key_first, (SAMPLES, width), 0, 1000, dtype=jnp.int32) < freq[None, :, field]).astype(jnp.int32)
        second = (jax.random.randint(key_second, (SAMPLES, width), 0, 1000, dtype=jnp.int32) < freq[None, :, field]).astype(jnp.int32)
        packed = packed + jnp.left_shift(first + second, 2 * field)
    return packed


def draw_sample_mask(key, part):
    key = jax.random.fold_in(key, 12)
    position = jnp.arange(SAMPLES, dtype=jnp.int32)
    limit = 300 + 600 * position // SAMPLES
    return (jax.random.randint(key, (SAMPLES,), 0, 1000, dtype=jnp.int32) < limit).astype(jnp.int32)


def levels(own_key, shape, pieces, smallest, high):
    factor_of = 1.0
    for dim, shards_of in pieces:
        draws = jax.random.uniform(jax.random.fold_in(jax.random.fold_in(own_key, 6), dim), (shards_of,), jnp.float32, smallest / len(pieces), high / len(pieces))
        factor_of = factor_of * jnp.repeat(jnp.exp(draws), shape[dim] // shards_of).reshape((-1,) + (1,) * (len(shape) - 1 - dim))
    return factor_of


def length_profile(amount, total, most, lean):
    portions = [(1 << 20) // math.isqrt(rank ** lean) + 1 for rank in range(2, amount + 1)]
    surplus, given = total - most - (amount - 1), [1] * (amount - 1)
    while surplus > 0:
        candidates = [i for i in range(amount - 1) if given[i] < most]
        pool, left = sum([portions[i] for i in candidates]), surplus
        for i in candidates:
            addition = min(most - given[i], max(1, left * portions[i] // pool), surplus)
            given[i] = given[i] + addition
            surplus = surplus - addition
    return np.array([most] + given)


def ragged(stream_key, number_of, total, bound, lean):
    if number_of == 2:
        one = jax.random.randint(stream_key, (), max(1, total - bound), min(bound, total - 1) + 1)
        return jnp.stack([one, total - one])
    sizes = jnp.asarray(length_profile(number_of, total, bound, lean), jnp.int32)
    twos = (number_of - 1) // 2
    giver, taker = sizes[1:1 + 2 * twos:2], sizes[2:2 + 2 * twos:2]
    slack = jnp.minimum(giver - 1, bound - taker)
    shifted = jax.random.randint(jax.random.fold_in(stream_key, 1), (twos,), 0, 1 << 20) % (slack + 1)
    sizes = sizes.at[1:1 + 2 * twos:2].set(giver - shifted).at[2:2 + 2 * twos:2].set(taker + shifted)
    return sizes[jax.random.permutation(jax.random.fold_in(stream_key, 2), number_of)]


def scatter_about(stream_key, dims, deviation, most, shards=(), kind=jnp.bfloat16):
    drawn = deviation * jax.random.normal(stream_key, dims, jnp.float32)
    if shards:
        drawn = drawn * levels(stream_key, dims, shards, -0.22, 0.18)
    return jnp.clip(drawn, -most, most).astype(kind)


def setup_inputs(seed: int = 0, part: int = 0) -> dict:
    key_list = jax.random.split(jax.random.key(seed), 6)
    part_splits = jax.random.split(jax.random.fold_in(key_list[5], part), 6)
    genotype = draw_genotype(jax.random.fold_in(jax.random.fold_in(key_list[5], part), 71), part)
    traits = scatter_about(part_splits[1], (SAMPLES, K), 1.0, 6.0, ((0, 4),))
    sample_mask = draw_sample_mask(jax.random.fold_in(jax.random.fold_in(key_list[5], part), 71), part)
    block_ids = jnp.searchsorted(jnp.cumsum(ragged(part_splits[3], BLOCKS, SNPS, SNPS - SNPS // 4, 0)), jnp.arange(SNPS), side="right").astype(jnp.int32)
    running_total = scatter_about(part_splits[4], (K, K), 1.0, 6.0, ((0, 16),), jnp.float32)
    return dict(genotype=genotype, traits=traits, sample_mask=sample_mask, block_ids=block_ids, running_total=running_total)


def unpack(words):
    shifts = 2 * lax.iota(jnp.int32, 4)
    values = words[:, :, None] >> shifts[None, None, :] & 3
    return values.reshape(words.shape[0], words.shape[1] * 4)

def reference(genotype, traits, sample_mask, block_ids, running_total):
    keep = sample_mask.astype(jnp.bfloat16)
    masked = traits * keep[:, None]
    count = jnp.sum(sample_mask.astype(jnp.float32))
    colsum = jnp.dot(keep[None, :], traits, preferred_element_type=jnp.float32)[0]
    width = SNP_DEV // 4

    def one_group(index):
        words = lax.dynamic_slice_in_dim(genotype, index * width, width, 1)
        dosage = unpack(words).astype(jnp.bfloat16)
        sums = jnp.dot(keep[None, :], dosage, preferred_element_type=jnp.float32)[0]
        squares = jnp.dot(keep[None, :], dosage * dosage, preferred_element_type=jnp.float32)[0]
        raw = jnp.dot(dosage.T, masked, preferred_element_type=jnp.float32)
        return (raw, sums, squares)
    indices = jnp.arange(N_SNPS).astype(jnp.int32)
    raw, sums, squares = lax.map(one_group, indices)
    raw = raw.reshape(SNPS, K)
    sums = sums.reshape(SNPS)
    squares = squares.reshape(SNPS)
    mean = sums / count
    var = squares / count - mean * mean
    scale = lax.rsqrt((var + 1e-05) * count)
    assoc = (raw - mean[:, None] * colsum[None, :]) * scale[:, None]
    rounded = assoc.astype(jnp.bfloat16)
    factor = 1.0 / math.sqrt(SNPS)
    grams = []
    for block in range(BLOCKS):
        select = (block_ids == block).astype(jnp.bfloat16)
        weighted = rounded * select[:, None]
        grams.append(jnp.dot(weighted.T, rounded, preferred_element_type=jnp.float32) * factor)
    block_gram = jnp.stack(grams)
    total = running_total + lax.optimization_barrier(jnp.sum(block_gram, axis=0))
    return (assoc.reshape(N_SNPS, SNP_DEV, K), block_gram, total)
```

```python
import functools
import math

import jax
import jax.numpy as jnp
from jax import lax
from jax.experimental import pallas as pl
from jax.experimental.pallas import tpu as pltpu
from jax.sharding import PartitionSpec as P

BLOCKS = 2


def unpack(words):
    shifts = 2 * lax.iota(jnp.int32, 4)
    values = words[:, :, None] >> shifts[None, None, :] & 3
    return values.reshape(words.shape[0], words.shape[1] * 4)


def shards(genotype, traits, sample_mask, block_ids, running_total):
    dosage = unpack(genotype).astype(jnp.bfloat16)
    keep = sample_mask.astype(jnp.bfloat16)
    masked = traits * keep[:, None]
    local_count = jnp.sum(sample_mask.astype(jnp.float32))
    local_colsum = jnp.dot(keep[None, :], traits, preferred_element_type=jnp.float32)[0]
    local_sums = jnp.dot(keep[None, :], dosage, preferred_element_type=jnp.float32)[0]
    local_squares = jnp.dot(keep[None, :], dosage * dosage, preferred_element_type=jnp.float32)[0]
    snp_count = dosage.shape[1]
    n_rows = snp_count // lax.axis_size("samples")
    offset = lax.axis_index("samples") * n_rows
    raw = lax.psum_scatter(
        lax.dot_general(
            dosage, masked, (((0,), (0,)), ((), ())), preferred_element_type=jnp.float32
        ),
        "samples",
        scatter_dimension=0,
        tiled=True,
    )
    count, colsum, sums, squares = lax.psum(
        (local_count, local_colsum, local_sums, local_squares), "samples"
    )
    sums = lax.dynamic_slice_in_dim(sums, offset, n_rows, 0)
    squares = lax.dynamic_slice_in_dim(squares, offset, n_rows, 0)
    mean = sums / count
    var = squares / count - mean * mean
    scale = lax.rsqrt((var + 1e-05) * count)
    assoc = (raw - mean[:, None] * colsum[None, :]) * scale[:, None]
    rounded = assoc.astype(jnp.bfloat16)
    factor = 1.0 / math.sqrt(snp_count * lax.axis_size("snps"))
    labels = lax.iota(jnp.int32, BLOCKS)
    own_ids = lax.dynamic_slice_in_dim(block_ids, offset, n_rows, 0)
    onehot = (labels[:, None] == own_ids[None, :]).astype(jnp.bfloat16)
    weighted = rounded[None, :, :] * onehot[:, :, None]
    partial_gram = jnp.einsum("brk,rl->bkl", weighted, rounded, preferred_element_type=jnp.float32)
    gram = lax.psum_scatter(partial_gram, ("samples", "snps"), scatter_dimension=1, tiled=True)
    block_gram = gram * factor
    total = running_total + jnp.sum(block_gram, axis=0)
    return (assoc[None, :, :], block_gram, total)


MESH = pl.DeviceIdType.MESH
F32 = jnp.float32


def kernel(
    n_snp_dev, factor, geno, traits, mask, ids, running, assoc, gram, total,
    words, lhs, y_own, q_send, q_recv, st_send, st_recv, z_buf, zt, mixed, g_own, g_send, g_recv,
    q_ss, q_rs, st_ss, st_rs, z_ss, z_rs, g_ss, g_rs,
):
    grp, s, p = (lax.axis_index(a) for a in ("groups", "samples", "snps"))
    ns = lax.axis_size("samples")
    n_samples, n_words = geno.shape
    wpd = n_words // ns
    rows = 4 * wpd
    traits_n = traits.shape[1]

    def along(k):
        return (grp, lax.rem(s + k, ns), p)

    def other(bit):
        return (grp, s, p + bit - 2 * bit * lax.rem(p // bit, 2))

    barrier = pltpu.get_barrier_semaphore()
    peers = [along(k) for k in range(1, ns)] + [other(1), other(2)]
    for peer in peers:
        pl.semaphore_signal(barrier, inc=1, device_id=peer, device_id_type=MESH)

    for i in range(n_samples // 128):
        block = geno[i * 128:(i + 1) * 128, :]
        block = jnp.concatenate([block, jnp.zeros((128, -n_words % 128), jnp.int32)], axis=1)
        words[:, i * 128:(i + 1) * 128] = block.T[:n_words] * mask[:, i * 128:(i + 1) * 128]
    count = jnp.sum(mask[...].astype(F32), axis=1, keepdims=True)
    lhs[rows:rows + 16, :] = jnp.broadcast_to(mask[...].astype(F32), (16, n_samples)).astype(jnp.bfloat16)

    pl.semaphore_wait(barrier, len(peers))

    def q_copy(k):
        return pltpu.make_async_remote_copy(
            q_send.at[k - 1], q_recv.at[k - 1], q_ss.at[k - 1], q_rs.at[k - 1],
            device_id=along(k), device_id_type=MESH)

    def st_copy(k):
        return pltpu.make_async_remote_copy(
            st_send.at[k - 1], st_recv.at[k - 1], st_ss.at[k - 1], st_rs.at[k - 1],
            device_id=along(k), device_id_type=MESH)

    lane = lax.broadcasted_iota(jnp.int32, (rows, 128), 1)
    sub = lax.broadcasted_iota(jnp.int32, (8, traits_n), 0)

    def one(k, carry):
        t = lax.rem(s + k, ns)
        w = words[pl.ds(pl.multiple_of(t * wpd, wpd), wpd), :]
        s1, s2 = [], []
        for f in range(4):
            d = ((w >> (2 * f)) & 3).astype(F32)
            s1.append(jnp.sum(d, axis=1, keepdims=True))
            s2.append(jnp.sum(d * d, axis=1, keepdims=True))
            lhs[f * wpd:(f + 1) * wpd, :] = d.astype(jnp.bfloat16)
        sums = jnp.concatenate(s1, axis=0)
        squares = jnp.concatenate(s2, axis=0)
        raw = jnp.dot(lhs[...], traits[...], preferred_element_type=F32)
        colsum = raw[rows:rows + 1]
        y = raw[:rows] - (sums / jnp.maximum(count, 1.0)) * colsum
        top = jnp.maximum(jnp.max(jnp.abs(y), axis=1, keepdims=True), 1e-30)
        y_own[...] = y
        q_send[k - 1] = jnp.round(y * (32767.0 / top)).astype(jnp.int32).astype(jnp.int16)
        cols = jnp.where(lane == 0, sums, jnp.where(lane == 1, squares, jnp.where(lane == 2, top * (1.0 / 32767.0), 0.0)))
        cols = jnp.concatenate([cols, jnp.zeros((-rows % 128, 128), F32)], axis=0).T[:8]
        cols = jnp.concatenate([cols, jnp.zeros((8, traits_n - cols.shape[1]), F32)], axis=1)
        st_send[k - 1] = jnp.where(sub == 3, colsum, jnp.where(sub == 4, count, cols))

        @pl.when(k < ns)
        def _():
            st_copy(k).start()
            q_copy(k).start()

        return carry

    lax.fori_loop(1, ns + 1, one, 0)

    padded = rows + (-rows % 128)

    def columns(st):
        tall = jnp.concatenate([st[:, :padded], jnp.zeros((120, padded), F32)], axis=0).T
        return tall[:rows, 0:1], tall[:rows, 1:2], tall[:rows, 2:3]

    own = st_send[ns - 1]
    parts = [(own, columns(own))]
    y = y_own[...]
    for k in range(1, ns):
        st_copy(k).wait_recv()
        st = st_recv[k - 1]
        cols = columns(st)
        parts.append((st, cols))
        q_copy(k).wait_recv()
        y = y + q_recv[k - 1].astype(jnp.int32).astype(F32) * cols[2]
    n = sum(st[4:5, 0:1] for st, _ in parts)
    mean = sum(c[0] for _, c in parts) / n
    var = sum(c[1] for _, c in parts) / n - mean * mean
    scale = lax.rsqrt((var + 1e-05) * n)
    for st, c in parts:
        y = y + (c[0] / jnp.maximum(st[4:5, 0:1], 1.0) - mean) * st[3:4]
    z = y * scale
    zb = z.astype(jnp.bfloat16)
    z_buf[0, 0:rows, :] = zb
    n0 = jnp.sum((ids[...] == 0).astype(F32), axis=1, keepdims=True)
    at = lax.broadcasted_iota(jnp.int32, (1, traits_n), 1)
    field = sum((at >= f * wpd).astype(jnp.int32) for f in range(1, 4))
    j = s * rows + 4 * (at - field * wpd) + field
    first = (j.astype(F32) < n0).astype(F32)
    z_buf[0, rows:rows + 16, :] = jnp.broadcast_to(first, (16, traits_n)).astype(jnp.bfloat16)

    def z_copy(src, dst, to):
        return pltpu.make_async_remote_copy(
            z_buf.at[src], z_buf.at[dst], z_ss.at[dst - 1], z_rs.at[dst - 1],
            device_id=to, device_id_type=MESH)

    far, near, relay = z_copy(0, 2, other(2)), z_copy(0, 1, other(1)), z_copy(2, 3, other(1))
    far.start()
    near.start()
    for c in range(traits_n // 128):
        for f in range(4):
            mixed[c, pl.ds(f, wpd, stride=4), :] = z[f * wpd:(f + 1) * wpd, c * 128:(c + 1) * 128]
        assoc[:, c * 128:(c + 1) * 128] = mixed[c]

    own_rows = running.shape[0]

    def gram_of(i, acc):
        zc = z_buf[i, 0:rows, :]
        zc = jnp.concatenate([zc, jnp.zeros((padded - rows, traits_n), jnp.bfloat16)], axis=0)
        zt[...] = zc.astype(F32).T
        left = [zt[pl.ds(pl.multiple_of((lax.rem(s + k, ns) * n_snp_dev + p) * own_rows, own_rows), own_rows), :] for k in range(1, ns + 1)]
        left = jnp.concatenate(left, axis=0)
        chosen = z_buf[i, rows:rows + 16, :].astype(F32)[0:1, :padded]
        both = jnp.concatenate([left * chosen, left * (1.0 - chosen)], axis=0).astype(jnp.bfloat16)
        new = jnp.dot(both, zc, preferred_element_type=F32)
        return new if acc is None else acc + new

    acc = gram_of(0, None)
    near.wait_recv()
    acc = gram_of(1, acc)
    far.wait_recv()
    relay.start()
    acc = gram_of(2, acc)
    relay.wait_recv()
    acc = gram_of(3, acc)

    def g_copy(k):
        return pltpu.make_async_remote_copy(
            g_send.at[k - 1], g_recv.at[k - 1], g_ss.at[k - 1], g_rs.at[k - 1],
            device_id=along(k), device_id_type=MESH)

    half = ns * own_rows
    for k in range(1, ns):
        for b in range(BLOCKS):
            lo = b * half + (k - 1) * own_rows
            g_send[k - 1, b] = acc[lo:lo + own_rows].astype(jnp.bfloat16)
        g_copy(k).start()
    for b in range(BLOCKS):
        lo = b * half + (ns - 1) * own_rows
        g_own[b] = acc[lo:lo + own_rows]
    out = g_own[...]
    for k in range(1, ns):
        g_copy(k).wait_recv()
        out = out + g_recv[k - 1].astype(F32)
    out = out * factor
    gram[...] = out
    total[...] = running[...] + (out[0] + out[1])
    for k in range(1, ns):
        q_copy(k).wait_send()
        st_copy(k).wait_send()
        g_copy(k).wait_send()
    for c in (far, near, relay):
        c.wait_send()


def fused(genotype, traits, sample_mask, block_ids, running_total):
    ns, np_ = lax.axis_size("samples"), lax.axis_size("snps")
    n_samples, n_words = genotype.shape
    k = traits.shape[1]
    rows = 4 * n_words // ns
    padded = rows + (-rows % 128)
    own = running_total.shape[0]
    factor = 1.0 / math.sqrt(4 * n_words * np_)
    vmem = pl.BlockSpec(memory_space=pltpu.VMEM)
    bf16, dma = jnp.bfloat16, pltpu.SemaphoreType.DMA
    assoc, gram, total = pl.pallas_call(
        functools.partial(kernel, np_, factor),
        out_shape=(
            jax.ShapeDtypeStruct((rows, k), F32),
            jax.ShapeDtypeStruct((BLOCKS, own, k), F32),
            jax.ShapeDtypeStruct((own, k), F32),
        ),
        in_specs=[vmem] * 5,
        out_specs=(vmem,) * 3,
        scratch_shapes=[
            pltpu.VMEM((n_words, n_samples), jnp.int32),
            pltpu.VMEM((rows + 16, n_samples), bf16),
            pltpu.VMEM((rows, k), F32),
            pltpu.VMEM((ns, rows, k), jnp.int16),
            pltpu.VMEM((ns - 1, rows, k), jnp.int16),
            pltpu.VMEM((ns, 8, k), F32),
            pltpu.VMEM((ns - 1, 8, k), F32),
            pltpu.VMEM((np_, rows + 16, k), bf16),
            pltpu.VMEM((k, padded), F32),
            pltpu.VMEM((k // 128, rows, 128), F32),
            pltpu.VMEM((BLOCKS, own, k), F32),
            pltpu.VMEM((ns - 1, BLOCKS, own, k), bf16),
            pltpu.VMEM((ns - 1, BLOCKS, own, k), bf16),
        ] + [dma((ns - 1,))] * 4 + [dma((3,))] * 2 + [dma((ns - 1,))] * 2,
        compiler_params=pltpu.CompilerParams(
            collective_id=0, has_side_effects=True, vmem_limit_bytes=48 * 1024 * 1024
        ),
    )(genotype, traits, sample_mask.reshape(1, -1), block_ids.reshape(1, -1), running_total)
    return assoc[None], gram, total


def body(genotype, traits, sample_mask, block_ids, running_total):
    args = (genotype, traits, sample_mask, block_ids, running_total)
    ns = lax.axis_size("samples")
    n_words = genotype.shape[1]
    whole_tiles = n_words % (16 * ns) == 0 and running_total.shape[0] % 32 == 0
    if lax.axis_size("snps") == 4 and 1 < ns <= 4 and whole_tiles and 4 * n_words // ns <= traits.shape[1]:
        return fused(*args)
    return shards(*args)


def solution(mesh):
    placed = (
        P(("groups", "samples"), "snps"),
        P(("groups", "samples"), None),
        P(("groups", "samples")),
        P(("groups", "snps")),
        P(("groups", "samples", "snps"), None),
    )
    return jax.shard_map(
        body,
        mesh=mesh,
        in_specs=placed,
        out_specs=(
            P("snps", ("groups", "samples"), None),
            P(None, ("groups", "samples", "snps"), None),
            P(("groups", "samples", "snps"), None),
        ),
        check_vma=False,
    )
```

```python
import functools
import math

import jax
import jax.numpy as jnp
from jax import lax
from jax.experimental import pallas as pl
from jax.experimental.pallas import tpu as pltpu
from jax.sharding import PartitionSpec as P

BLOCKS = 2


def unpack(words):
    shifts = 2 * lax.iota(jnp.int32, 4)
    values = words[:, :, None] >> shifts[None, None, :] & 3
    return values.reshape(words.shape[0], words.shape[1] * 4)


def shards(genotype, traits, sample_mask, block_ids, running_total):
    dosage = unpack(genotype).astype(jnp.bfloat16)
    keep = sample_mask.astype(jnp.bfloat16)
    masked = traits * keep[:, None]
    local_count = jnp.sum(sample_mask.astype(jnp.float32))
    local_colsum = jnp.dot(keep[None, :], traits, preferred_element_type=jnp.float32)[0]
    local_sums = jnp.dot(keep[None, :], dosage, preferred_element_type=jnp.float32)[0]
    local_squares = jnp.dot(keep[None, :], dosage * dosage, preferred_element_type=jnp.float32)[0]
    snp_count = dosage.shape[1]
    n_rows = snp_count // lax.axis_size("samples")
    offset = lax.axis_index("samples") * n_rows
    raw = lax.psum_scatter(
        lax.dot_general(
            dosage, masked, (((0,), (0,)), ((), ())), preferred_element_type=jnp.float32
        ),
        "samples",
        scatter_dimension=0,
        tiled=True,
    )
    count, colsum, sums, squares = lax.psum(
        (local_count, local_colsum, local_sums, local_squares), "samples"
    )
    sums = lax.dynamic_slice_in_dim(sums, offset, n_rows, 0)
    squares = lax.dynamic_slice_in_dim(squares, offset, n_rows, 0)
    mean = sums / count
    var = squares / count - mean * mean
    scale = lax.rsqrt((var + 1e-05) * count)
    assoc = (raw - mean[:, None] * colsum[None, :]) * scale[:, None]
    rounded = assoc.astype(jnp.bfloat16)
    factor = 1.0 / math.sqrt(snp_count * lax.axis_size("snps"))
    labels = lax.iota(jnp.int32, BLOCKS)
    own_ids = lax.dynamic_slice_in_dim(block_ids, offset, n_rows, 0)
    onehot = (labels[:, None] == own_ids[None, :]).astype(jnp.bfloat16)
    weighted = rounded[None, :, :] * onehot[:, :, None]
    partial_gram = jnp.einsum("brk,rl->bkl", weighted, rounded, preferred_element_type=jnp.float32)
    gram = lax.psum_scatter(partial_gram, ("samples", "snps"), scatter_dimension=1, tiled=True)
    block_gram = gram * factor
    total = running_total + jnp.sum(block_gram, axis=0)
    return (assoc[None, :, :], block_gram, total)


MESH = pl.DeviceIdType.MESH
F32 = jnp.float32
BF16 = jnp.bfloat16
PW = 16
PR = 4 * PW


def kernel(
    n_snp_dev, factor, geno, traits_hbm, mask, ids, running, assoc, gram, total,
    words, traits, lhs, y_own, q_send, q_recv, st_send, st_recv, n_buf, z_buf, zt, mixed, g_own, g_send, g_recv,
    in_sem, q_ss, q_rs, st_ss, st_rs, n_ss, n_rs, z_ss, z_rs, g_ss, g_rs,
):
    grp, s, p = (lax.axis_index(a) for a in ("groups", "samples", "snps"))
    ns = lax.axis_size("samples")
    n_words, n_samples = words.shape
    wpd = n_words // ns
    pieces = wpd // PW
    rows = 4 * wpd
    width = traits.shape[1]

    geno_in = pltpu.make_async_copy(geno, words, in_sem.at[0])
    traits_in = pltpu.make_async_copy(traits_hbm, traits, in_sem.at[1])
    geno_in.start()
    traits_in.start()

    def along(k):
        return (grp, lax.rem(s + k, ns), p)

    def flip(bit):
        return bit - 2 * bit * lax.rem(p // bit, 2)

    def other(x):
        return (grp, s, p + sum(flip(b) for b in (1, 2) if x & b))

    barrier = pltpu.get_barrier_semaphore()
    peers = [along(k) for k in range(1, ns)] + [other(x) for x in range(1, 4)]
    for peer in peers:
        pl.semaphore_signal(barrier, inc=1, device_id=peer, device_id_type=MESH)

    keep = mask[...]
    count = jnp.sum(keep.astype(F32), axis=1, keepdims=True)
    lhs[ns * PR:, :] = jnp.broadcast_to(keep.astype(F32), (16, n_samples)).astype(BF16)
    n0 = jnp.sum((ids[...] == 0).astype(F32), axis=1, keepdims=True)
    n_buf[0] = jnp.broadcast_to(n0, n_buf.shape[1:])

    def remote(src, dst, ss, rs, to):
        return pltpu.make_async_remote_copy(src, dst, ss, rs, device_id=to, device_id_type=MESH)

    def q_copy(c, k):
        return remote(q_send.at[c, k - 1], q_recv.at[c, k - 1], q_ss.at[c, k - 1], q_rs.at[c, k - 1], along(k))

    def st_copy(c, k):
        return remote(st_send.at[c, k - 1], st_recv.at[c, k - 1], st_ss.at[c, k - 1], st_rs.at[c, k - 1], along(k))

    def n_copy(x):
        return remote(n_buf.at[0], n_buf.at[x], n_ss.at[x - 1], n_rs.at[x - 1], other(x))

    def z_copy(c, src, dst, x):
        return remote(
            z_buf.at[c, pl.ds(src * PR, PR)], z_buf.at[c, pl.ds(dst * PR, PR)],
            z_ss.at[c, dst - 1], z_rs.at[c, dst - 1], other(x))

    def far(c):
        return z_copy(c, 0, 2, 2)

    def near(c):
        return z_copy(c, 0, 1, 1)

    def relay(c):
        return z_copy(c, 2, 3, 1)

    def g_copy(k):
        return remote(g_send.at[k - 1], g_recv.at[k - 1], g_ss.at[k - 1], g_rs.at[k - 1], along(k))

    pl.semaphore_wait(barrier, len(peers))
    for x in range(1, 4):
        n_copy(x).start()
    geno_in.wait()
    lane = lax.broadcasted_iota(jnp.int32, (PR, 128), 1)
    sub = lax.broadcasted_iota(jnp.int32, (8, 128), 0)

    def one(c, carry):
        stats = []
        for k in range(1, ns + 1):
            t = lax.rem(s + k, ns)
            w = words[pl.ds(pl.multiple_of(t * wpd + c * PW, PW), PW), :] * keep
            s1, s2 = [], []
            for f in range(4):
                d = ((w >> (2 * f)) & 3).astype(F32)
                s1.append(jnp.sum(d, axis=1, keepdims=True))
                s2.append(jnp.sum(d * d, axis=1, keepdims=True))
                at = (k - 1) * PR + f * PW
                lhs[at:at + PW, :] = d.astype(BF16)
            stats.append((jnp.concatenate(s1, axis=0), jnp.concatenate(s2, axis=0)))

        @pl.when(c == 0)
        def _():
            traits_in.wait()

        raw = jnp.dot(lhs[...], traits[...], preferred_element_type=F32)
        colsum = raw[ns * PR:ns * PR + 1]
        tail = jnp.concatenate(
            [jnp.zeros((3, 128), F32)] + [colsum[:, i * 128:(i + 1) * 128] for i in range(4)]
            + [jnp.broadcast_to(count, (1, 128))], axis=0)
        for k in range(1, ns + 1):
            sums, squares = stats[k - 1]
            y = raw[(k - 1) * PR:k * PR] - (sums / jnp.maximum(count, 1.0)) * colsum
            top = jnp.maximum(jnp.max(jnp.abs(y), axis=1, keepdims=True), 1e-30)
            if k < ns:
                q_send[c, k - 1] = jnp.round(y * (32767.0 / top)).astype(jnp.int32).astype(jnp.int16)
            else:
                y_own[c] = y
            cols = jnp.where(lane == 0, sums, jnp.where(lane == 1, squares, top * (1.0 / 32767.0)))
            cols = jnp.concatenate([cols, jnp.zeros((128 - PR, 128), F32)], axis=0).T[:8]
            st_send[c, k - 1] = jnp.where(sub < 3, cols, tail)
            if k < ns:
                st_copy(c, k).start()
                q_copy(c, k).start()
        return carry

    lax.fori_loop(0, pieces, one, 0)

    def columns(st):
        tall = jnp.concatenate([st, jnp.zeros((120, 128), F32)], axis=0).T
        return tall[:PR, 0:1], tall[:PR, 1:2], tall[:PR, 2:3]

    def standardise(c):
        st = st_send[c, ns - 1]
        parts = [(st, columns(st))]
        y = y_own[c]
        for k in range(1, ns):
            st_copy(c, k).wait_recv()
            st = st_recv[c, k - 1]
            cols = columns(st)
            parts.append((st, cols))
            q_copy(c, k).wait_recv()
            y = y + q_recv[c, k - 1].astype(jnp.int32).astype(F32) * cols[2]
        n = sum(st[7:8, 0:1] for st, _ in parts)
        mean = sum(cols[0] for _, cols in parts) / n
        var = sum(cols[1] for _, cols in parts) / n - mean * mean
        scale = lax.rsqrt((var + 1e-05) * n)
        for st, cols in parts:
            colsum = jnp.concatenate([st[i:i + 1] for i in range(3, 7)], axis=1)
            y = y + (cols[0] / jnp.maximum(st[7:8, 0:1], 1.0) - mean) * colsum
        z = y * scale
        z_buf[c, 0:PR, :] = z.astype(BF16)
        far(c).start()
        near(c).start()
        for i in range(width // 128):
            for f in range(4):
                mixed[i, pl.ds(c * PR + f, PW, stride=4), :] = z[f * PW:(f + 1) * PW, i * 128:(i + 1) * 128]
            assoc[c * PR:(c + 1) * PR, i * 128:(i + 1) * 128] = mixed[i, c * PR:(c + 1) * PR, :]

    own_rows = running.shape[0]
    lanes = lax.broadcasted_iota(jnp.int32, (1, 4 * PR), 1)
    slot = lanes // PR
    snp = s * rows + 4 * lax.rem(lanes, PW) + lax.rem(lanes, PR) // PW

    def limits():
        for x in range(1, 4):
            n_copy(x).wait_recv()
        return sum(jnp.where(slot == x, n_buf[x, 0:1, 0:1], 0.0) for x in range(4))

    def gram_of(c, limit):
        near(c).wait_recv()
        relay(c).wait_recv()
        zc = z_buf[c]
        zt[...] = zc.astype(F32).T
        left = jnp.concatenate([
            zt[pl.ds(pl.multiple_of((lax.rem(s + k, ns) * n_snp_dev + p) * own_rows, own_rows), own_rows), :]
            for k in range(1, ns + 1)], axis=0)
        chosen = ((snp + c * PR).astype(F32) < limit).astype(F32)
        both = jnp.concatenate([left * chosen, left * (1.0 - chosen)], axis=0).astype(BF16)
        return jnp.dot(both, zc, preferred_element_type=F32)

    acc, limit = 0.0, None
    for c in range(pieces):
        standardise(c)
        if c >= 1:
            far(c - 1).wait_recv()
            relay(c - 1).start()
        if c >= 2:
            limit = limits() if limit is None else limit
            acc = acc + gram_of(c - 2, limit)
    far(pieces - 1).wait_recv()
    relay(pieces - 1).start()
    limit = limits() if limit is None else limit
    for c in range(max(pieces - 2, 0), pieces):
        acc = acc + gram_of(c, limit)

    half = ns * own_rows
    for k in range(1, ns):
        for b in range(BLOCKS):
            lo = b * half + (k - 1) * own_rows
            g_send[k - 1, b] = acc[lo:lo + own_rows].astype(BF16)
        g_copy(k).start()
    for b in range(BLOCKS):
        lo = b * half + (ns - 1) * own_rows
        g_own[b] = acc[lo:lo + own_rows]
    out = g_own[...]
    for k in range(1, ns):
        g_copy(k).wait_recv()
        out = out + g_recv[k - 1].astype(F32)
    out = out * factor
    gram[...] = out
    total[...] = running[...] + (out[0] + out[1])
    for c in range(pieces):
        for k in range(1, ns):
            q_copy(c, k).wait_send()
            st_copy(c, k).wait_send()
        for copy in (far(c), near(c), relay(c)):
            copy.wait_send()
    for k in range(1, ns):
        g_copy(k).wait_send()
    for x in range(1, 4):
        n_copy(x).wait_send()


def store(*refs):
    n = len(refs) // 2
    sems = refs[-1]
    copies = [pltpu.make_async_copy(refs[i], refs[n + i], sems.at[i]) for i in range(n)]
    for copy in copies:
        copy.start()
    for copy in copies:
        copy.wait()


def fused(genotype, traits, sample_mask, block_ids, running_total):
    ns, np_ = lax.axis_size("samples"), lax.axis_size("snps")
    n_samples, n_words = genotype.shape
    k = traits.shape[1]
    rows = 4 * n_words // ns
    pieces = rows // PR
    own = running_total.shape[0]
    factor = 1.0 / math.sqrt(4 * n_words * np_)
    vmem = pl.BlockSpec(memory_space=pltpu.VMEM)
    hbm = pl.BlockSpec(memory_space=pltpu.HBM)
    dma = pltpu.SemaphoreType.DMA
    shapes = (
        jax.ShapeDtypeStruct((rows, k), F32),
        jax.ShapeDtypeStruct((BLOCKS, own, k), F32),
        jax.ShapeDtypeStruct((own, k), F32),
    )
    results = pl.pallas_call(
        functools.partial(kernel, np_, factor),
        out_shape=shapes,
        in_specs=[hbm, hbm, vmem, vmem, vmem],
        out_specs=(vmem,) * 3,
        scratch_shapes=[
            pltpu.VMEM((n_words, n_samples), jnp.int32),
            pltpu.VMEM((n_samples, k), BF16),
            pltpu.VMEM((ns * PR + 16, n_samples), BF16),
            pltpu.VMEM((pieces, PR, k), F32),
            pltpu.VMEM((pieces, ns - 1, PR, k), jnp.int16),
            pltpu.VMEM((pieces, ns - 1, PR, k), jnp.int16),
            pltpu.VMEM((pieces, ns, 8, 128), F32),
            pltpu.VMEM((pieces, ns - 1, 8, 128), F32),
            pltpu.VMEM((4, 8, 128), F32),
            pltpu.VMEM((pieces, 4 * PR, k), BF16),
            pltpu.VMEM((k, 4 * PR), F32),
            pltpu.VMEM((k // 128, rows, 128), F32),
            pltpu.VMEM((BLOCKS, own, k), F32),
            pltpu.VMEM((ns - 1, BLOCKS, own, k), BF16),
            pltpu.VMEM((ns - 1, BLOCKS, own, k), BF16),
            dma((2,)),
        ] + [dma((pieces, ns - 1))] * 4 + [dma((3,))] * 2 + [dma((pieces, 3))] * 2 + [dma((ns - 1,))] * 2,
        compiler_params=pltpu.CompilerParams(
            collective_id=0, has_side_effects=True, vmem_limit_bytes=40 * 1024 * 1024
        ),
    )(genotype.T, traits, sample_mask.reshape(1, -1), block_ids.reshape(1, -1), running_total)
    assoc, gram, total = pl.pallas_call(
        store, out_shape=shapes, in_specs=[vmem] * 3, out_specs=(hbm,) * 3, scratch_shapes=[dma((3,))],
    )(*results)
    return assoc[None], gram, total


def body(genotype, traits, sample_mask, block_ids, running_total):
    args = (genotype, traits, sample_mask, block_ids, running_total)
    ns = lax.axis_size("samples")
    whole_tiles = genotype.shape[1] % (PW * ns) == 0 and running_total.shape[0] % 32 == 0
    if lax.axis_size("snps") == 4 and ns == 4 and whole_tiles and traits.shape[1] == 512:
        return fused(*args)
    return shards(*args)


def solution(mesh):
    placed = (
        P(("groups", "samples"), "snps"),
        P(("groups", "samples"), None),
        P(("groups", "samples")),
        P(("groups", "snps")),
        P(("groups", "samples", "snps"), None),
    )
    return jax.shard_map(
        body,
        mesh=mesh,
        in_specs=placed,
        out_specs=(
            P("snps", ("groups", "samples"), None),
            P(None, ("groups", "samples", "snps"), None),
            P(("groups", "samples", "snps"), None),
        ),
        check_vma=False,
    )
```

```python
import functools
import math

import jax
import jax.numpy as jnp
from jax import lax
from jax.experimental import pallas as pl
from jax.experimental.pallas import tpu as pltpu
from jax.sharding import PartitionSpec as P

BLOCKS = 2


def unpack(words):
    shifts = 2 * lax.iota(jnp.int32, 4)
    values = words[:, :, None] >> shifts[None, None, :] & 3
    return values.reshape(words.shape[0], words.shape[1] * 4)


def shards(genotype, traits, sample_mask, block_ids, running_total):
    dosage = unpack(genotype).astype(jnp.bfloat16)
    keep = sample_mask.astype(jnp.bfloat16)
    masked = traits * keep[:, None]
    local_count = jnp.sum(sample_mask.astype(jnp.float32))
    local_colsum = jnp.dot(keep[None, :], traits, preferred_element_type=jnp.float32)[0]
    local_sums = jnp.dot(keep[None, :], dosage, preferred_element_type=jnp.float32)[0]
    local_squares = jnp.dot(keep[None, :], dosage * dosage, preferred_element_type=jnp.float32)[0]
    snp_count = dosage.shape[1]
    n_rows = snp_count // lax.axis_size("samples")
    offset = lax.axis_index("samples") * n_rows
    raw = lax.psum_scatter(
        lax.dot_general(
            dosage, masked, (((0,), (0,)), ((), ())), preferred_element_type=jnp.float32
        ),
        "samples",
        scatter_dimension=0,
        tiled=True,
    )
    count, colsum, sums, squares = lax.psum(
        (local_count, local_colsum, local_sums, local_squares), "samples"
    )
    sums = lax.dynamic_slice_in_dim(sums, offset, n_rows, 0)
    squares = lax.dynamic_slice_in_dim(squares, offset, n_rows, 0)
    mean = sums / count
    var = squares / count - mean * mean
    scale = lax.rsqrt((var + 1e-05) * count)
    assoc = (raw - mean[:, None] * colsum[None, :]) * scale[:, None]
    rounded = assoc.astype(jnp.bfloat16)
    factor = 1.0 / math.sqrt(snp_count * lax.axis_size("snps"))
    labels = lax.iota(jnp.int32, BLOCKS)
    own_ids = lax.dynamic_slice_in_dim(block_ids, offset, n_rows, 0)
    onehot = (labels[:, None] == own_ids[None, :]).astype(jnp.bfloat16)
    weighted = rounded[None, :, :] * onehot[:, :, None]
    partial_gram = jnp.einsum("brk,rl->bkl", weighted, rounded, preferred_element_type=jnp.float32)
    gram = lax.psum_scatter(partial_gram, ("samples", "snps"), scatter_dimension=1, tiled=True)
    block_gram = gram * factor
    total = running_total + jnp.sum(block_gram, axis=0)
    return (assoc[None, :, :], block_gram, total)


MESH = pl.DeviceIdType.MESH
F32 = jnp.float32
BF16 = jnp.bfloat16
PW = 16
PR = 4 * PW


def kernel(
    n_snp_dev, factor, geno, traits_hbm, mask_hbm, ids_hbm, assoc, gram,
    words, traits, mask, ids, lhs, y_own, y_far, q_send, q_recv, st_send, st_recv, r_send, r_recv, rs_send, rs_recv, n_buf, z_buf, zt, mixed, g_own, g_send, g_recv,
    in_sem, r_ss, r_rs, rt_ss, rt_rs, q_ss, q_rs, st_ss, st_rs, n_ss, n_rs, z_ss, z_rs, g_ss, g_rs,
):
    grp, s, p = (lax.axis_index(a) for a in ("groups", "samples", "snps"))
    ns = lax.axis_size("samples")
    n_words, n_samples = words.shape
    wpd = n_words // ns
    pieces = wpd // PW
    rows = 4 * wpd
    width = traits.shape[1]

    geno_in = pltpu.make_async_copy(geno, words, in_sem.at[0])
    traits_in = pltpu.make_async_copy(traits_hbm, traits, in_sem.at[1])
    small_in = [
        pltpu.make_async_copy(src, dst, in_sem.at[2 + i])
        for i, (src, dst) in enumerate(((mask_hbm, mask), (ids_hbm, ids)))]
    small_in[0].start()
    geno_in.start()
    traits_in.start()
    small_in[1].start()

    def along(k):
        return (grp, lax.rem(s + k, ns), p)

    def flip(bit):
        return bit - 2 * bit * lax.rem(p // bit, 2)

    def other(x):
        return (grp, s, p + sum(flip(b) for b in (1, 2) if x & b))

    barrier = pltpu.get_barrier_semaphore()
    peers = [along(k) for k in range(1, ns)] + [other(x) for x in range(1, 4)]
    for peer in peers:
        pl.semaphore_signal(barrier, inc=1, device_id=peer, device_id_type=MESH)

    small_in[0].wait()
    keep = mask[...]
    count = jnp.sum(keep.astype(F32), axis=1, keepdims=True)
    lhs[ns * PR:, :] = jnp.broadcast_to(keep.astype(F32), (16, n_samples)).astype(BF16)

    def remote(src, dst, ss, rs, to):
        return pltpu.make_async_remote_copy(src, dst, ss, rs, device_id=to, device_id_type=MESH)

    def q_copy(c, k):
        return remote(q_send.at[c, k - 1], q_recv.at[c, k - 1], q_ss.at[c, k - 1], q_rs.at[c, k - 1], along(k))

    def st_copy(c, k):
        return remote(st_send.at[c, k - 1], st_recv.at[c, k - 1], st_ss.at[c, k - 1], st_rs.at[c, k - 1], along(k))

    def n_copy(x):
        return remote(n_buf.at[0], n_buf.at[x], n_ss.at[x - 1], n_rs.at[x - 1], other(x))

    def z_copy(c, src, dst, x):
        return remote(
            z_buf.at[c, pl.ds(src * PR, PR)], z_buf.at[c, pl.ds(dst * PR, PR)],
            z_ss.at[c, dst - 1], z_rs.at[c, dst - 1], other(x))

    def far(c):
        return z_copy(c, 0, 2, 2)

    def near(c):
        return z_copy(c, 0, 1, 1)

    def relay(c):
        return z_copy(c, 2, 3, 1)

    def g_copy(k):
        return remote(g_send.at[k - 1], g_recv.at[k - 1], g_ss.at[k - 1], g_rs.at[k - 1], along(k))

    geno_in.wait()
    lane = lax.broadcasted_iota(jnp.int32, (PR, 128), 1)
    sub = lax.broadcasted_iota(jnp.int32, (8, 128), 0)

    edge = (s == 0) | (s == ns - 1)
    inner = jnp.logical_not(edge)
    relayed = range(pieces - 1)

    def skips(k, sending):
        first, last = (ns - 1, 1) if sending else (1, ns - 1)
        return ((s == 0) & (k == first)) | ((s == ns - 1) & (k == last))

    def r_copy(c):
        return remote(r_send.at[c], r_recv.at[c], r_ss.at[c], r_rs.at[c], (grp, s + 1 - 2 * lax.rem(s, 2), p))

    def rt_copy(c):
        return remote(rs_send.at[c], rs_recv.at[c], rt_ss.at[c], rt_rs.at[c], (grp, s + 1 - 2 * lax.rem(s, 2), p))

    def tall(tile):
        return jnp.concatenate([tile, jnp.zeros((120, 128), F32)], axis=0).T

    def flat(column):
        wide = jnp.concatenate([jnp.broadcast_to(column, (PR, 128)), jnp.zeros((128 - PR, 128), F32)], axis=0)
        return wide.T[:8]

    def fixed(y):
        top = jnp.maximum(jnp.max(jnp.abs(y), axis=1, keepdims=True), 1e-30)
        return jnp.round(y * (32767.0 / top)).astype(jnp.int32).astype(jnp.int16), top * (1.0 / 32767.0)

    def compute(c):
        stats = []
        for k in range(1, ns + 1):
            t = lax.rem(s + k, ns)
            w = words[pl.ds(pl.multiple_of(t * wpd + c * PW, PW), PW), :] * keep
            s1, s2 = [], []
            for f in range(4):
                d = ((w >> (2 * f)) & 3).astype(F32)
                s1.append(jnp.sum(d, axis=1, keepdims=True))
                s2.append(jnp.sum(d * d, axis=1, keepdims=True))
                at = (k - 1) * PR + f * PW
                lhs[at:at + PW, :] = d.astype(BF16)
            stats.append((jnp.concatenate(s1, axis=0), jnp.concatenate(s2, axis=0)))
        if c == 0:
            traits_in.wait()
        raw = jnp.dot(lhs[...], traits[...], preferred_element_type=F32)
        colsum = raw[ns * PR:ns * PR + 1]
        tail = jnp.concatenate(
            [jnp.zeros((3, 128), F32)] + [colsum[:, i * 128:(i + 1) * 128] for i in range(4)]
            + [jnp.broadcast_to(count, (1, 128))], axis=0)
        for k in range(1, ns + 1):
            sums, squares = stats[k - 1]
            y = raw[(k - 1) * PR:k * PR] - (sums / jnp.maximum(count, 1.0)) * colsum
            unit = jnp.zeros((PR, 1), F32)
            if k < ns:
                q_send[c, k - 1], unit = fixed(y)
                if k == 2 and c in relayed:
                    y_far[c] = y
                if k != 2 and c in relayed:
                    @pl.when(skips(k, True))
                    def _(k=k, unit=unit):
                        r_send[c] = q_send[c, k - 1]
                        rs_send[c] = flat(unit)
            else:
                y_own[c] = y
            cols = jnp.where(lane == 0, sums, jnp.where(lane == 1, squares, unit))
            cols = jnp.concatenate([cols, jnp.zeros((128 - PR, 128), F32)], axis=0).T[:8]
            st_send[c, k - 1] = jnp.where(sub < 3, cols, tail)

    def send(c):
        if c in relayed:
            @pl.when(edge)
            def _():
                rt_copy(c).start()
                r_copy(c).start()
        for k in (2, 1, 3):
            if c in relayed:
                if k == 2:
                    ready = edge
                    st_ready = edge
                else:
                    ready = jnp.logical_not(skips(k, True))
                    st_ready = None
            else:
                ready = st_ready = None
            if st_ready is None:
                st_copy(c, k).start()
            else:
                pl.when(st_ready)(st_copy(c, k).start)
            if ready is None:
                q_copy(c, k).start()
            else:
                pl.when(ready)(q_copy(c, k).start)

    def pass_on(c):
        @pl.when(inner)
        def _():
            rt_copy(c).wait_recv()
            r_copy(c).wait_recv()
            theirs = tall(rs_recv[c])[:PR, 0:1]
            q, unit = fixed(y_far[c] + r_recv[c].astype(jnp.int32).astype(F32) * theirs)
            q_send[c, 1] = q
            st_send[c, 1] = jnp.where(sub == 2, flat(unit), st_send[c, 1])
            st_copy(c, 2).start()
            q_copy(c, 2).start()

    for c in range(pieces):
        compute(c)
        if c == 0:
            pl.semaphore_wait(barrier, len(peers))
        send(c)
        if c >= 1 and c - 1 in relayed:
            pass_on(c - 1)
    small_in[1].wait()
    n0 = jnp.sum((ids[...].reshape(1, -1) == 0).astype(F32), axis=1, keepdims=True)
    n_buf[0] = jnp.broadcast_to(n0, n_buf.shape[1:])
    for x in range(1, 4):
        n_copy(x).start()

    def columns(st):
        wide = tall(st)
        return wide[:PR, 0:1], wide[:PR, 1:2], wide[:PR, 2:3]

    def standardise(c):
        st = st_send[c, ns - 1]
        parts = [(st, columns(st))]
        for k in range(1, ns):
            st_copy(c, k).wait_recv()
            st = st_recv[c, k - 1]
            cols = columns(st)
            parts.append((st, cols))

            def add(k=k, unit=cols[2]):
                q_copy(c, k).wait_recv()
                y_own[c] += q_recv[c, k - 1].astype(jnp.int32).astype(F32) * unit

            if c in relayed and k != 2:
                pl.when(jnp.logical_not(skips(k, False)))(add)
            else:
                add()
        y = y_own[c]
        n = sum(st[7:8, 0:1] for st, _ in parts)
        mean = sum(cols[0] for _, cols in parts) / n
        var = sum(cols[1] for _, cols in parts) / n - mean * mean
        scale = lax.rsqrt((var + 1e-05) * n)
        for st, cols in parts:
            colsum = jnp.concatenate([st[i:i + 1] for i in range(3, 7)], axis=1)
            y = y + (cols[0] / jnp.maximum(st[7:8, 0:1], 1.0) - mean) * colsum
        z = y * scale
        z_buf[c, 0:PR, :] = z.astype(BF16)
        far(c).start()
        near(c).start()
        for i in range(width // 128):
            for f in range(4):
                mixed[i, pl.ds(c * PR + f, PW, stride=4), :] = z[f * PW:(f + 1) * PW, i * 128:(i + 1) * 128]
            assoc[c * PR:(c + 1) * PR, i * 128:(i + 1) * 128] = mixed[i, c * PR:(c + 1) * PR, :]

    own_rows = gram.shape[1]
    lanes = lax.broadcasted_iota(jnp.int32, (1, 4 * PR), 1)
    slot = lanes // PR
    snp = s * rows + 4 * lax.rem(lanes, PW) + lax.rem(lanes, PR) // PW

    def limits():
        for x in range(1, 4):
            n_copy(x).wait_recv()
        return sum(jnp.where(slot == x, n_buf[x, 0:1, 0:1], 0.0) for x in range(4))

    def gram_of(c, limit):
        near(c).wait_recv()
        relay(c).wait_recv()
        zc = z_buf[c]
        zt[...] = zc.astype(F32).T
        left = jnp.concatenate([
            zt[pl.ds(pl.multiple_of((lax.rem(s + k, ns) * n_snp_dev + p) * own_rows, own_rows), own_rows), :]
            for k in range(1, ns + 1)], axis=0)
        chosen = ((snp + c * PR).astype(F32) < limit).astype(F32)
        both = jnp.concatenate([left * chosen, left * (1.0 - chosen)], axis=0).astype(BF16)
        return jnp.dot(both, zc, preferred_element_type=F32)

    acc, limit = 0.0, None
    for c in range(pieces):
        standardise(c)
        if c >= 1:
            far(c - 1).wait_recv()
            relay(c - 1).start()
        if c >= 2:
            limit = limits() if limit is None else limit
            acc = acc + gram_of(c - 2, limit)
    far(pieces - 1).wait_recv()
    relay(pieces - 1).start()
    limit = limits() if limit is None else limit
    for c in range(max(pieces - 2, 0), pieces):
        acc = acc + gram_of(c, limit)

    half = ns * own_rows
    for k in range(1, ns):
        for b in range(BLOCKS):
            lo = b * half + (k - 1) * own_rows
            g_send[k - 1, b] = acc[lo:lo + own_rows].astype(BF16)
        g_copy(k).start()
    for b in range(BLOCKS):
        lo = b * half + (ns - 1) * own_rows
        g_own[b] = acc[lo:lo + own_rows]
    out = g_own[...]
    for k in range(1, ns):
        g_copy(k).wait_recv()
        out = out + g_recv[k - 1].astype(F32)
    out = out * factor
    gram[...] = out
    for c in range(pieces):
        for k in range(1, ns):
            st_copy(c, k).wait_send()
            if c in relayed and k != 2:
                pl.when(jnp.logical_not(skips(k, True)))(q_copy(c, k).wait_send)
            else:
                q_copy(c, k).wait_send()
        for copy in (far(c), near(c), relay(c)):
            copy.wait_send()
    for c in relayed:
        @pl.when(edge)
        def _(c=c):
            r_copy(c).wait_send()
            rt_copy(c).wait_send()
    for k in range(1, ns):
        g_copy(k).wait_send()
    for x in range(1, 4):
        n_copy(x).wait_send()


def fused(genotype, traits, sample_mask, block_ids, running_total):
    ns, np_ = lax.axis_size("samples"), lax.axis_size("snps")
    n_samples, n_words = genotype.shape
    k = traits.shape[1]
    rows = 4 * n_words // ns
    pieces = rows // PR
    own = running_total.shape[0]
    factor = 1.0 / math.sqrt(4 * n_words * np_)
    vmem = pl.BlockSpec(memory_space=pltpu.VMEM)
    hbm = pl.BlockSpec(memory_space=pl.ANY)
    dma = pltpu.SemaphoreType.DMA
    shapes = (
        jax.ShapeDtypeStruct((rows, k), F32),
        jax.ShapeDtypeStruct((BLOCKS, own, k), F32),
    )
    results = pl.pallas_call(
        functools.partial(kernel, np_, factor),
        out_shape=shapes,
        in_specs=[hbm] * 4,
        out_specs=(vmem,) * 2,
        scratch_shapes=[
            pltpu.VMEM((n_words, n_samples), jnp.int32),
            pltpu.VMEM((n_samples, k), BF16),
            pltpu.VMEM((1, n_samples), jnp.int32),
            pltpu.VMEM(block_ids.shape, jnp.int32),
            pltpu.VMEM((ns * PR + 16, n_samples), BF16),
            pltpu.VMEM((pieces, PR, k), F32),
            pltpu.VMEM((pieces, PR, k), F32),
            pltpu.VMEM((pieces, ns - 1, PR, k), jnp.int16),
            pltpu.VMEM((pieces, ns - 1, PR, k), jnp.int16),
            pltpu.VMEM((pieces, ns, 8, 128), F32),
            pltpu.VMEM((pieces, ns - 1, 8, 128), F32),
            pltpu.VMEM((pieces, PR, k), jnp.int16),
            pltpu.VMEM((pieces, PR, k), jnp.int16),
            pltpu.VMEM((pieces, 8, 128), F32),
            pltpu.VMEM((pieces, 8, 128), F32),
            pltpu.VMEM((4, 8, 128), F32),
            pltpu.VMEM((pieces, 4 * PR, k), BF16),
            pltpu.VMEM((k, 4 * PR), F32),
            pltpu.VMEM((k // 128, rows, 128), F32),
            pltpu.VMEM((BLOCKS, own, k), F32),
            pltpu.VMEM((ns - 1, BLOCKS, own, k), BF16),
            pltpu.VMEM((ns - 1, BLOCKS, own, k), BF16),
            dma((4,)),
        ] + [dma((pieces,))] * 4 + [dma((pieces, ns - 1))] * 4 + [dma((3,))] * 2 + [dma((pieces, 3))] * 2 + [dma((ns - 1,))] * 2,
        compiler_params=pltpu.CompilerParams(
            collective_id=0, has_side_effects=True, vmem_limit_bytes=52 * 1024 * 1024
        ),
    )(genotype.T, traits, sample_mask.reshape(1, -1), block_ids)
    assoc, gram = results
    return assoc[None], gram, running_total + jnp.sum(gram, axis=0)


def body(genotype, traits, sample_mask, block_ids, running_total):
    args = (genotype, traits, sample_mask, block_ids, running_total)
    ns = lax.axis_size("samples")
    whole_tiles = genotype.shape[1] % (PW * ns) == 0 and running_total.shape[0] % 32 == 0
    if lax.axis_size("snps") == 4 and ns == 4 and whole_tiles and traits.shape[1] == 512:
        return fused(*args)
    return shards(*args)


def solution(mesh):
    placed = (
        P(("groups", "samples"), "snps"),
        P(("groups", "samples"), None),
        P(("groups", "samples")),
        P(("groups", "snps")),
        P(("groups", "samples", "snps"), None),
    )
    return jax.shard_map(
        body,
        mesh=mesh,
        in_specs=placed,
        out_specs=(
            P("snps", ("groups", "samples"), None),
            P(None, ("groups", "samples", "snps"), None),
            P(("groups", "samples", "snps"), None),
        ),
        check_vma=False,
    )
```

```python
import functools
import math

import jax
import jax.numpy as jnp
from jax import lax
from jax.experimental import pallas as pl
from jax.experimental.pallas import tpu as pltpu
from jax.sharding import PartitionSpec as P

BLOCKS = 2


def unpack(words):
    shifts = 2 * lax.iota(jnp.int32, 4)
    values = words[:, :, None] >> shifts[None, None, :] & 3
    return values.reshape(words.shape[0], words.shape[1] * 4)


def shards(genotype, traits, sample_mask, block_ids, running_total):
    dosage = unpack(genotype).astype(jnp.bfloat16)
    keep = sample_mask.astype(jnp.bfloat16)
    masked = traits * keep[:, None]
    local_count = jnp.sum(sample_mask.astype(jnp.float32))
    local_colsum = jnp.dot(keep[None, :], traits, preferred_element_type=jnp.float32)[0]
    local_sums = jnp.dot(keep[None, :], dosage, preferred_element_type=jnp.float32)[0]
    local_squares = jnp.dot(keep[None, :], dosage * dosage, preferred_element_type=jnp.float32)[0]
    snp_count = dosage.shape[1]
    n_rows = snp_count // lax.axis_size("samples")
    offset = lax.axis_index("samples") * n_rows
    raw = lax.psum_scatter(
        lax.dot_general(
            dosage, masked, (((0,), (0,)), ((), ())), preferred_element_type=jnp.float32
        ),
        "samples",
        scatter_dimension=0,
        tiled=True,
    )
    count, colsum, sums, squares = lax.psum(
        (local_count, local_colsum, local_sums, local_squares), "samples"
    )
    sums = lax.dynamic_slice_in_dim(sums, offset, n_rows, 0)
    squares = lax.dynamic_slice_in_dim(squares, offset, n_rows, 0)
    mean = sums / count
    var = squares / count - mean * mean
    scale = lax.rsqrt((var + 1e-05) * count)
    assoc = (raw - mean[:, None] * colsum[None, :]) * scale[:, None]
    rounded = assoc.astype(jnp.bfloat16)
    factor = 1.0 / math.sqrt(snp_count * lax.axis_size("snps"))
    labels = lax.iota(jnp.int32, BLOCKS)
    own_ids = lax.dynamic_slice_in_dim(block_ids, offset, n_rows, 0)
    onehot = (labels[:, None] == own_ids[None, :]).astype(jnp.bfloat16)
    weighted = rounded[None, :, :] * onehot[:, :, None]
    partial_gram = jnp.einsum("brk,rl->bkl", weighted, rounded, preferred_element_type=jnp.float32)
    gram = lax.psum_scatter(partial_gram, ("samples", "snps"), scatter_dimension=1, tiled=True)
    block_gram = gram * factor
    total = running_total + jnp.sum(block_gram, axis=0)
    return (assoc[None, :, :], block_gram, total)


MESH = pl.DeviceIdType.MESH
F32 = jnp.float32
BF16 = jnp.bfloat16
PW = 16
PR = 4 * PW


def kernel(
    n_snp_dev, factor, geno, traits_hbm, small_hbm, assoc, gram,
    words, traits, mask, ids, lhs, y_own, y_far, q_send, q_recv, st_send, st_recv, r_send, r_recv, rs_send, rs_recv, n_buf, z_buf, zt, mixed, g_own, g_send, g_recv,
    in_sem, r_ss, r_rs, rt_ss, rt_rs, q_ss, q_rs, st_ss, st_rs, n_ss, n_rs, z_ss, z_rs, g_ss, g_rs,
):
    grp, s, p = (lax.axis_index(a) for a in ("groups", "samples", "snps"))
    ns = lax.axis_size("samples")
    n_words, n_samples = words.shape
    wpd = n_words // ns
    pieces = wpd // PW
    rows = 4 * wpd
    width = traits.shape[1]

    geno_in = pltpu.make_async_copy(geno, words, in_sem.at[0])
    traits_in = pltpu.make_async_copy(traits_hbm, traits, in_sem.at[1])
    small_in = [
        pltpu.make_async_copy(small_hbm.at[pl.ds(0, n_samples)], mask, in_sem.at[2]),
        pltpu.make_async_copy(small_hbm.at[pl.ds(n_samples, ids.shape[0])], ids, in_sem.at[3]),
    ]
    small_in[0].start()
    geno_in.start()
    traits_in.start()
    small_in[1].start()

    def along(k):
        return (grp, lax.rem(s + k, ns), p)

    def flip(bit):
        return bit - 2 * bit * lax.rem(p // bit, 2)

    def other(x):
        return (grp, s, p + sum(flip(b) for b in (1, 2) if x & b))

    barrier = pltpu.get_barrier_semaphore()
    peers = [along(k) for k in range(1, ns)] + [other(x) for x in range(1, 4)]
    for peer in peers:
        pl.semaphore_signal(barrier, inc=1, device_id=peer, device_id_type=MESH)

    small_in[0].wait()
    keep = mask[...].reshape(1, -1)
    keep_bits = -keep
    count = jnp.sum(keep.astype(F32), axis=1, keepdims=True)
    lhs[ns * PR:, :] = jnp.broadcast_to(keep.astype(F32), (16, n_samples)).astype(BF16)

    def remote(src, dst, ss, rs, to):
        return pltpu.make_async_remote_copy(src, dst, ss, rs, device_id=to, device_id_type=MESH)

    def q_copy(c, k):
        return remote(q_send.at[c, k - 1], q_recv.at[c, k - 1], q_ss.at[c, k - 1], q_rs.at[c, k - 1], along(k))

    def st_copy(c, k):
        return remote(st_send.at[c, k - 1], st_recv.at[c, k - 1], st_ss.at[c, k - 1], st_rs.at[c, k - 1], along(k))

    def n_copy(x):
        return remote(n_buf.at[0], n_buf.at[x], n_ss.at[x - 1], n_rs.at[x - 1], other(x))

    def z_copy(c, src, dst, x):
        return remote(
            z_buf.at[c, pl.ds(src * PR, PR)], z_buf.at[c, pl.ds(dst * PR, PR)],
            z_ss.at[c, dst - 1], z_rs.at[c, dst - 1], other(x))

    def far(c):
        return z_copy(c, 0, 2, 2)

    def near(c):
        return z_copy(c, 0, 1, 1)

    def relay(c):
        return z_copy(c, 2, 3, 1)

    def g_copy(k):
        return remote(g_send.at[k - 1], g_recv.at[k - 1], g_ss.at[k - 1], g_rs.at[k - 1], along(k))

    geno_in.wait()
    lane = lax.broadcasted_iota(jnp.int32, (PR, 128), 1)
    sub = lax.broadcasted_iota(jnp.int32, (8, 128), 0)

    edge = (s == 0) | (s == ns - 1)
    inner = jnp.logical_not(edge)
    relayed = range(pieces - 1)

    def skips(k, sending):
        first, last = (ns - 1, 1) if sending else (1, ns - 1)
        return ((s == 0) & (k == first)) | ((s == ns - 1) & (k == last))

    def r_copy(c):
        return remote(r_send.at[c], r_recv.at[c], r_ss.at[c], r_rs.at[c], (grp, s + 1 - 2 * lax.rem(s, 2), p))

    def rt_copy(c):
        return remote(rs_send.at[c], rs_recv.at[c], rt_ss.at[c], rt_rs.at[c], (grp, s + 1 - 2 * lax.rem(s, 2), p))

    def tall(tile):
        return jnp.concatenate([tile, jnp.zeros((120, 128), F32)], axis=0).T

    def flat(column):
        wide = jnp.concatenate([jnp.broadcast_to(column, (PR, 128)), jnp.zeros((128 - PR, 128), F32)], axis=0)
        return wide.T[:8]

    def fixed(y):
        top = jnp.maximum(jnp.max(jnp.abs(y), axis=1, keepdims=True), 1e-30)
        return jnp.round(y * (32767.0 / top)).astype(jnp.int32).astype(jnp.int16), top * (1.0 / 32767.0)

    def compute(c):
        stats = []
        for k in range(1, ns + 1):
            t = lax.rem(s + k, ns)
            w = words[pl.ds(pl.multiple_of(t * wpd + c * PW, PW), PW), :] & keep_bits
            s1, s2 = [], []
            for f in range(4):
                d = ((w >> (2 * f)) & 3).astype(F32).astype(BF16)
                parts = [d[:, i:i + 128] for i in range(0, n_samples, 128)]
                s1.append(jnp.sum(functools.reduce(jnp.add, parts).astype(F32), axis=1, keepdims=True))
                s2.append(jnp.sum(functools.reduce(jnp.add, [v * v for v in parts]).astype(F32), axis=1, keepdims=True))
                at = (k - 1) * PR + f * PW
                lhs[at:at + PW, :] = d
            stats.append((jnp.concatenate(s1, axis=0), jnp.concatenate(s2, axis=0)))
        if c == 0:
            traits_in.wait()
        raw = jnp.dot(lhs[...], traits[...], preferred_element_type=F32)
        colsum = raw[ns * PR:ns * PR + 1]
        tail = jnp.concatenate(
            [jnp.zeros((3, 128), F32)] + [colsum[:, i * 128:(i + 1) * 128] for i in range(4)]
            + [jnp.broadcast_to(count, (1, 128))], axis=0)
        for k in range(1, ns + 1):
            sums, squares = stats[k - 1]
            y = raw[(k - 1) * PR:k * PR] - (sums / jnp.maximum(count, 1.0)) * colsum
            unit = jnp.zeros((PR, 1), F32)
            if k < ns:
                q_send[c, k - 1], unit = fixed(y)
                if k == 2 and c in relayed:
                    y_far[c] = y
                if k != 2 and c in relayed:
                    @pl.when(skips(k, True))
                    def _(k=k, unit=unit):
                        r_send[c] = q_send[c, k - 1]
                        rs_send[c] = flat(unit)
            else:
                y_own[c] = y
            cols = jnp.where(lane == 0, sums, jnp.where(lane == 1, squares, unit))
            cols = jnp.concatenate([cols, jnp.zeros((128 - PR, 128), F32)], axis=0).T[:8]
            st_send[c, k - 1] = jnp.where(sub < 3, cols, tail)

    inward, upper = lax.rem(s + 1, ns) // 2, s // 2
    first = inward * 2 + (1 - inward) * (3 - 2 * upper)
    second = (1 - inward) * 2 + inward * (1 + 2 * upper)
    ordered = (first, second, 6 - first - second)

    def send(c):
        if c in relayed:
            @pl.when(edge)
            def _():
                rt_copy(c).start()
                r_copy(c).start()
                st_copy(c, first).start()
        for k in ordered[1:] if c in relayed else ordered:
            st_copy(c, k).start()
            q_copy(c, k).start()

    def pass_on(c):
        @pl.when(inner)
        def _():
            rt_copy(c).wait_recv()
            r_copy(c).wait_recv()
            theirs = tall(rs_recv[c])[:PR, 0:1]
            q, unit = fixed(y_far[c] + r_recv[c].astype(jnp.int32).astype(F32) * theirs)
            q_send[c, 1] = q
            st_send[c, 1] = jnp.where(sub == 2, flat(unit), st_send[c, 1])
            st_copy(c, 2).start()
            q_copy(c, 2).start()

    for c in range(pieces):
        compute(c)
        if c == 0:
            pl.semaphore_wait(barrier, len(peers))
        send(c)
        if c >= 1 and c - 1 in relayed:
            pass_on(c - 1)
    small_in[1].wait()
    n0 = jnp.sum((ids[...].reshape(1, -1) == 0).astype(F32), axis=1, keepdims=True)
    n_buf[0] = jnp.broadcast_to(n0, n_buf.shape[1:])
    for x in range(1, 4):
        n_copy(x).start()

    def columns(st):
        wide = tall(st)
        return wide[:PR, 0:1], wide[:PR, 1:2], wide[:PR, 2:3]

    def standardise(c):
        st = st_send[c, ns - 1]
        parts = [(st, columns(st))]
        for k in range(1, ns):
            st_copy(c, k).wait_recv()
            st = st_recv[c, k - 1]
            cols = columns(st)
            parts.append((st, cols))

            def add(k=k, unit=cols[2]):
                q_copy(c, k).wait_recv()
                y_own[c] += q_recv[c, k - 1].astype(jnp.int32).astype(F32) * unit

            if c in relayed and k != 2:
                pl.when(jnp.logical_not(skips(k, False)))(add)
            else:
                add()
        y = y_own[c]
        n = sum(st[7:8, 0:1] for st, _ in parts)
        mean = sum(cols[0] for _, cols in parts) / n
        var = sum(cols[1] for _, cols in parts) / n - mean * mean
        scale = lax.rsqrt((var + 1e-05) * n)
        for st, cols in parts:
            colsum = jnp.concatenate([st[i:i + 1] for i in range(3, 7)], axis=1)
            y = y + (cols[0] / jnp.maximum(st[7:8, 0:1], 1.0) - mean) * colsum
        z = y * scale
        z_buf[c, 0:PR, :] = z.astype(BF16)
        far(c).start()
        near(c).start()
        for i in range(width // 128):
            for f in range(4):
                mixed[i, pl.ds(c * PR + f, PW, stride=4), :] = z[f * PW:(f + 1) * PW, i * 128:(i + 1) * 128]
            assoc[c * PR:(c + 1) * PR, i * 128:(i + 1) * 128] = mixed[i, c * PR:(c + 1) * PR, :]

    own_rows = gram.shape[1]
    lanes = lax.broadcasted_iota(jnp.int32, (1, 4 * PR), 1)
    slot = lanes // PR
    snp = s * rows + 4 * lax.rem(lanes, PW) + lax.rem(lanes, PR) // PW

    def limits():
        for x in range(1, 4):
            n_copy(x).wait_recv()
        return sum(jnp.where(slot == x, n_buf[x, 0:1, 0:1], 0.0) for x in range(4))

    def gram_of(c, limit):
        near(c).wait_recv()
        relay(c).wait_recv()
        zc = z_buf[c]
        zt[...] = zc.astype(F32).T
        left = jnp.concatenate([
            zt[pl.ds(pl.multiple_of((lax.rem(s + k, ns) * n_snp_dev + p) * own_rows, own_rows), own_rows), :]
            for k in range(1, ns + 1)], axis=0)
        chosen = ((snp + c * PR).astype(F32) < limit).astype(F32)
        both = jnp.concatenate([left * chosen, left * (1.0 - chosen)], axis=0).astype(BF16)
        return jnp.dot(both, zc, preferred_element_type=F32)

    acc, limit = 0.0, None
    for c in range(pieces):
        standardise(c)
        if c >= 1:
            far(c - 1).wait_recv()
            relay(c - 1).start()
        if c >= 2:
            limit = limits() if limit is None else limit
            acc = acc + gram_of(c - 2, limit)
    far(pieces - 1).wait_recv()
    relay(pieces - 1).start()
    limit = limits() if limit is None else limit
    for c in range(max(pieces - 2, 0), pieces):
        acc = acc + gram_of(c, limit)

    half = ns * own_rows
    for k in range(1, ns):
        for b in range(BLOCKS):
            lo = b * half + (k - 1) * own_rows
            g_send[k - 1, b] = acc[lo:lo + own_rows].astype(BF16)
    for k in ordered:
        g_copy(k).start()
    for b in range(BLOCKS):
        lo = b * half + (ns - 1) * own_rows
        g_own[b] = acc[lo:lo + own_rows]
    out = g_own[...]
    for k in range(1, ns):
        g_copy(k).wait_recv()
        out = out + g_recv[k - 1].astype(F32)
    out = out * factor
    gram[...] = out
    for c in range(pieces):
        for k in range(1, ns):
            st_copy(c, k).wait_send()
            if c in relayed and k != 2:
                pl.when(jnp.logical_not(skips(k, True)))(q_copy(c, k).wait_send)
            else:
                q_copy(c, k).wait_send()
        for copy in (far(c), near(c), relay(c)):
            copy.wait_send()
    for c in relayed:
        @pl.when(edge)
        def _(c=c):
            r_copy(c).wait_send()
            rt_copy(c).wait_send()
    for k in range(1, ns):
        g_copy(k).wait_send()
    for x in range(1, 4):
        n_copy(x).wait_send()


def fused(genotype, traits, sample_mask, block_ids, running_total):
    ns, np_ = lax.axis_size("samples"), lax.axis_size("snps")
    n_samples, n_words = genotype.shape
    k = traits.shape[1]
    rows = 4 * n_words // ns
    pieces = rows // PR
    own = running_total.shape[0]
    factor = 1.0 / math.sqrt(4 * n_words * np_)
    vmem = pl.BlockSpec(memory_space=pltpu.VMEM)
    hbm = pl.BlockSpec(memory_space=pl.ANY)
    dma = pltpu.SemaphoreType.DMA
    shapes = (
        jax.ShapeDtypeStruct((rows, k), F32),
        jax.ShapeDtypeStruct((BLOCKS, own, k), F32),
    )
    results = pl.pallas_call(
        functools.partial(kernel, np_, factor),
        out_shape=shapes,
        in_specs=[hbm] * 3,
        out_specs=(vmem,) * 2,
        scratch_shapes=[
            pltpu.VMEM((n_words, n_samples), jnp.int32),
            pltpu.VMEM((n_samples, k), BF16),
            pltpu.VMEM((n_samples,), jnp.int32),
            pltpu.VMEM(block_ids.shape, jnp.int32),
            pltpu.VMEM((ns * PR + 16, n_samples), BF16),
            pltpu.VMEM((pieces, PR, k), F32),
            pltpu.VMEM((pieces, PR, k), F32),
            pltpu.VMEM((pieces, ns - 1, PR, k), jnp.int16),
            pltpu.VMEM((pieces, ns - 1, PR, k), jnp.int16),
            pltpu.VMEM((pieces, ns, 8, 128), F32),
            pltpu.VMEM((pieces, ns - 1, 8, 128), F32),
            pltpu.VMEM((pieces, PR, k), jnp.int16),
            pltpu.VMEM((pieces, PR, k), jnp.int16),
            pltpu.VMEM((pieces, 8, 128), F32),
            pltpu.VMEM((pieces, 8, 128), F32),
            pltpu.VMEM((4, 8, 128), F32),
            pltpu.VMEM((pieces, 4 * PR, k), BF16),
            pltpu.VMEM((k, 4 * PR), F32),
            pltpu.VMEM((k // 128, rows, 128), F32),
            pltpu.VMEM((BLOCKS, own, k), F32),
            pltpu.VMEM((ns - 1, BLOCKS, own, k), BF16),
            pltpu.VMEM((ns - 1, BLOCKS, own, k), BF16),
            dma((4,)),
        ] + [dma((pieces,))] * 4 + [dma((pieces, ns - 1))] * 4 + [dma((3,))] * 2 + [dma((pieces, 3))] * 2 + [dma((ns - 1,))] * 2,
        compiler_params=pltpu.CompilerParams(
            collective_id=0, has_side_effects=True, vmem_limit_bytes=52 * 1024 * 1024
        ),
    )(genotype.T, traits, jnp.concatenate([sample_mask, block_ids]))
    assoc, gram = results
    return assoc[None], gram, running_total + jnp.sum(gram, axis=0)


def body(genotype, traits, sample_mask, block_ids, running_total):
    args = (genotype, traits, sample_mask, block_ids, running_total)
    ns = lax.axis_size("samples")
    whole_tiles = genotype.shape[0] % 128 == 0 and genotype.shape[0] <= 8192 and genotype.shape[1] % (PW * ns) == 0 and running_total.shape[0] % 32 == 0
    if lax.axis_size("snps") == 4 and ns == 4 and whole_tiles and traits.shape[1] == 512:
        return fused(*args)
    return shards(*args)


def solution(mesh):
    placed = (
        P(("groups", "samples"), "snps"),
        P(("groups", "samples"), None),
        P(("groups", "samples")),
        P(("groups", "snps")),
        P(("groups", "samples", "snps"), None),
    )
    return jax.shard_map(
        body,
        mesh=mesh,
        in_specs=placed,
        out_specs=(
            P("snps", ("groups", "samples"), None),
            P(None, ("groups", "samples", "snps"), None),
            P(("groups", "samples", "snps"), None),
        ),
        check_vma=False,
    )
```
